32 devices in a mesh: rep: 2 (over y), wide: 8 (over z, x), narrow: 2 (over core).
Axes of the slice: x: 2, y: 2, z: 4, core: 2. Of those that a mesh axis runs over, the one named last changes fastest.
Arguments:
- hidden_rows: bfloat16 [128, 16384], P(('rep', 'wide'), 'narrow'), parts along dimension 0, may hold values from -600 to 600, as said below
- query_weight: bfloat16 [16384, 16384], P('narrow', 'wide'), may hold values from -0.046875 to 0.046875
- key_value_weight: bfloat16 [16384, 2048], P('narrow', 'wide'), may hold values from -0.046875 to 0.046875
- cache_keys: bfloat16 [128, 192, 1024], P(('rep', 'wide', 'narrow')), parts along dimension 0, may hold values from -200 to 200, as said below
- earlier_values: bfloat16 [128, 192, 1024], P(('rep', 'wide', 'narrow')), parts along dimension 0, may hold values from -6 to 6
- lengths: int32 [128], P(('rep', 'wide', 'narrow')), parts along dimension 0, may hold values from 1 to 192, as said below
- positions: int32 [128], P(('rep', 'wide', 'narrow')), parts along dimension 0, may hold values from 0 to 8191
Outputs:
- attended: bfloat16 [128, 16384], P(('rep', 'wide', 'narrow')), parts along dimension 0
The draws below stay inside these ranges and needn't reach their ends.
There are 2 independent parts, one for each index of `rep`. The reference program is written for one: setup_inputs(seed, part) draws one part's arguments, and reference() takes and returns one part's arrays. A program takes and returns all parts, laid end to end along the dimension named above; an argument that names none is the same for every part. Nothing has to cross between parts.
Inputs may be any that keep to these rules, and one draw needn't show every extreme that they name: `hidden_rows`: entries are finite. `cache_keys`: entries are finite. `lengths`: some row has all 192 slots live.
All inputs are finite; a program needn't handle non-finite values.
Results may differ from the reference program's by a relative error of at most 0.00455.
The reference program's roundings to bfloat16 on the way count: a program that leaves them out, or rounds other values in their place, can miss the bound.
Values may be sent and summed in bfloat16 or wider, within the bound.
A program may use at most 128 MiB of HBM per device.

```python
import jax
import jax.numpy as jnp
from jax import lax

MODEL_WIDTH = 16384
HQ = 128
KEY_VALUE_HEADS = 8
HEAD_WIDTH = 128
CACHE_SLOTS = 192
BATCH_ROWS = 64


def draw_hidden_rows(key, part):
    key = jax.random.fold_in(key, 11)
    random_key_root, key_rows, key_cols = jax.random.split(key, 3)
    random_base = jnp.clip(jax.random.normal(random_key_root, (BATCH_ROWS, MODEL_WIDTH), jnp.float32), -6.0, 6.0)
    row_scale = jnp.exp(jax.random.uniform(key_rows, (BATCH_ROWS, 1), jnp.float32, 0.0, jnp.log(10.0)))
    col_scale = jnp.exp(jax.random.uniform(key_cols, (1, MODEL_WIDTH), jnp.float32, 0.0, jnp.log(10.0)))
    return (random_base * row_scale * col_scale).astype(jnp.bfloat16)


def draw_cache_keys(key, part):
    key = jax.random.fold_in(key, 23)
    random_key_root = jax.random.fold_in(key, 0)
    random_base = jnp.clip(jax.random.normal(random_key_root, (BATCH_ROWS, CACHE_SLOTS, KEY_VALUE_HEADS * HEAD_WIDTH), jnp.float32), -6.0, 6.0)
    return random_base.astype(jnp.bfloat16)


def draw_lengths(key, part):
    key = jax.random.fold_in(key, 37)
    key_lens, key_full = jax.random.split(key, 2)
    drawn = jax.random.randint(key_lens, (BATCH_ROWS,), 1, CACHE_SLOTS + 1)
    longest = jax.random.randint(key_full, (), 0, BATCH_ROWS)
    return jnp.where(jnp.arange(BATCH_ROWS) == longest, CACHE_SLOTS, drawn).astype(jnp.int32)


def plant(entries, stream_key, low, top_value):
    spot = [jax.random.randint(jax.random.fold_in(stream_key, axis), (), 0, length) for axis, length in enumerate(entries.shape)]
    main_axis = entries.shape.index(max(entries.shape))
    beside = spot[:main_axis] + [(spot[main_axis] + 1) % entries.shape[main_axis]] + spot[main_axis + 1:]
    return entries.at[tuple(spot)].set(low).at[tuple(beside)].set(top_value)


def levels(rng, dims, cuts, low, top_value):
    factor_of, own = 1.0, jax.random.fold_in(rng, 6)
    for position, parts in cuts:
        draws = jnp.exp(jax.random.uniform(jax.random.fold_in(own, position), (parts,), jnp.float32, low / len(cuts), top_value / len(cuts)))
        factor_of = factor_of * jnp.repeat(draws, dims[position] // parts).reshape([-1 if axis == position else 1 for axis in range(len(dims))])
    return factor_of


def scatter_about(rng, dims, deviation, most, pieces=(), held_as=jnp.bfloat16):
    result = deviation * jax.random.normal(rng, dims, jnp.float32)
    if pieces:
        result = result * levels(rng, dims, pieces, -0.22, 0.18)
    return jnp.clip(result, -most, most).astype(held_as)


def setup_inputs(seed: int = 0, part: int = 0) -> dict:
    seeds = jax.random.split(jax.random.key(seed), 8)
    part_keys = jax.random.split(jax.random.fold_in(seeds[7], part), 8)
    hidden_rows = draw_hidden_rows(jax.random.fold_in(jax.random.fold_in(seeds[7], part), 71), part)
    query_weight = scatter_about(seeds[1], (MODEL_WIDTH, HQ * HEAD_WIDTH), MODEL_WIDTH ** -0.5, 0.046875, ((0, 2), (1, 8)))
    key_value_weight = scatter_about(seeds[2], (MODEL_WIDTH, 2 * KEY_VALUE_HEADS * HEAD_WIDTH), MODEL_WIDTH ** -0.5, 0.046875, ((0, 2), (1, 8)))
    cache_keys = draw_cache_keys(jax.random.fold_in(jax.random.fold_in(seeds[7], part), 71), part)
    earlier_values = scatter_about(part_keys[4], (BATCH_ROWS, CACHE_SLOTS, KEY_VALUE_HEADS * HEAD_WIDTH), 1.0, 6.0, ((0, 16),))
    lengths = draw_lengths(jax.random.fold_in(jax.random.fold_in(seeds[7], part), 71), part)
    positions = plant(jax.random.randint(part_keys[6], (BATCH_ROWS,), 0, 8192), jax.random.fold_in(part_keys[6], 1), 0, 8191).astype(jnp.int32)
    return dict(hidden_rows=hidden_rows, query_weight=query_weight, key_value_weight=key_value_weight, cache_keys=cache_keys, earlier_values=earlier_values, lengths=lengths, positions=positions)


EPSILON = 1e-05

def rotate(values, positions):
    middle = values.shape[-1] // 2
    frequency = 500000.0 ** (-(jnp.arange(middle).astype(jnp.float32) * 2.0 / values.shape[-1]))
    angles = positions.astype(jnp.float32)[:, None] * frequency[None, :]
    cosine = jnp.cos(angles)[:, None, :]
    sine_part = jnp.sin(angles)[:, None, :]
    leading = values[..., :middle]
    trailing = values[..., middle:]
    return jnp.concatenate([leading * cosine - trailing * sine_part, trailing * cosine + leading * sine_part], axis=-1)

def attend(queries, new_pair, cached_keys, cached_values, lengths, positions):
    row_count, head_count, head_size = queries.shape
    kv_heads = cached_keys.shape[-1] // head_size
    group_size = head_count // kv_heads
    rotated = rotate(queries.astype(jnp.float32), positions).astype(jnp.bfloat16)
    split_pair = new_pair.reshape(row_count, kv_heads, 2, head_size)
    new_key = rotate(split_pair[:, :, 0, :].astype(jnp.float32), positions).astype(jnp.bfloat16)
    new_value = split_pair[:, :, 1, :]
    grouped = rotated.reshape(row_count, kv_heads, group_size, head_size).astype(jnp.float32)
    key_blocks = cached_keys.reshape(row_count, -1, kv_heads, head_size).astype(jnp.float32)
    value_blocks = cached_values.reshape(row_count, -1, kv_heads, head_size).astype(jnp.float32)
    scaling = head_size ** (-0.5)
    scores = jnp.einsum('rhgd,rchd->rhgc', grouped, key_blocks) * scaling
    own_score = jnp.einsum('rhgd,rhd->rhg', grouped, new_key.astype(jnp.float32)) * scaling
    live_mask = (jnp.arange(key_blocks.shape[1])[None, :] < lengths[:, None])[:, None, None, :]
    masked = jnp.where(live_mask, scores, -1e+30)
    peak_score = jnp.maximum(lax.optimization_barrier(jnp.max(masked, axis=-1)), own_score)
    weights = jnp.where(live_mask, jnp.exp(masked - peak_score[..., None]), 0.0)
    own_weight = jnp.exp(own_score - peak_score)
    totals = lax.optimization_barrier(jnp.sum(weights, axis=-1)) + own_weight
    rounded = weights.astype(jnp.bfloat16).astype(jnp.float32)
    own_rounded = own_weight.astype(jnp.bfloat16).astype(jnp.float32)
    blended = jnp.einsum('rhgc,rchd->rhgd', rounded, value_blocks)
    blended = blended + own_rounded[..., None] * new_value.astype(jnp.float32)[:, :, None, :]
    return (blended / totals[..., None]).reshape(row_count, head_count * head_size).astype(jnp.bfloat16)

def reference(hidden_rows, query_weight, key_value_weight, cache_keys, earlier_values, lengths, positions):
    widened = hidden_rows.astype(jnp.float32)
    squares = lax.optimization_barrier(jnp.sum(widened * widened, axis=1))
    normed = (widened * lax.rsqrt(squares / MODEL_WIDTH + EPSILON)[:, None]).astype(jnp.bfloat16)
    queries = jnp.dot(normed, query_weight, preferred_element_type=jnp.float32).astype(jnp.bfloat16)
    queries = queries.reshape(BATCH_ROWS, HQ, HEAD_WIDTH)
    new_pair = jnp.dot(normed, key_value_weight, preferred_element_type=jnp.float32).astype(jnp.bfloat16)

    def single_row(record):
        one_query, one_pair, one_keys, one_values, one_length, one_position = record
        return attend(one_query[None], one_pair[None], one_keys[None], one_values[None], one_length[None], one_position[None])[0]
    return lax.map(single_row, (queries, new_pair, cache_keys, earlier_values, lengths, positions))
```

```python
import functools

import jax
import jax.numpy as jnp
import numpy as np
from jax import lax
from jax.experimental import pallas as pl
from jax.experimental.pallas import tpu as pltpu
from jax.sharding import PartitionSpec as P

MODEL_WIDTH = 16384
HEAD_WIDTH = 128


EPSILON = 1e-05


def rotate(values, positions):
    middle = values.shape[-1] // 2
    frequency = 500000.0 ** (-(jnp.arange(middle).astype(jnp.float32) * 2.0 / values.shape[-1]))
    angles = positions.astype(jnp.float32)[:, None] * frequency[None, :]
    cosine = jnp.cos(angles)[:, None, :]
    sine_part = jnp.sin(angles)[:, None, :]
    leading = values[..., :middle]
    trailing = values[..., middle:]
    return jnp.concatenate(
        [leading * cosine - trailing * sine_part, trailing * cosine + leading * sine_part], axis=-1
    )


def attend(queries, new_pair, cached_keys, cached_values, lengths, positions):
    row_count, head_count, head_size = queries.shape
    kv_heads = cached_keys.shape[-1] // head_size
    group_size = head_count // kv_heads
    rotated = rotate(queries.astype(jnp.float32), positions).astype(jnp.bfloat16)
    split_pair = new_pair.reshape(row_count, kv_heads, 2, head_size)
    new_key = rotate(split_pair[:, :, 0, :].astype(jnp.float32), positions).astype(jnp.bfloat16)
    new_value = split_pair[:, :, 1, :]
    grouped = rotated.reshape(row_count, kv_heads, group_size, head_size)
    key_blocks = cached_keys.reshape(row_count, -1, kv_heads, head_size)
    value_blocks = cached_values.reshape(row_count, -1, kv_heads, head_size)
    scaling = head_size ** (-0.5)
    scores = (
        jnp.einsum("rhgd,rchd->rhgc", grouped, key_blocks, preferred_element_type=jnp.float32)
        * scaling
    )
    own_score = (
        jnp.einsum("rhgd,rhd->rhg", grouped, new_key, preferred_element_type=jnp.float32) * scaling
    )
    live_mask = (jnp.arange(key_blocks.shape[1])[None, :] < lengths[:, None])[:, None, None, :]
    masked = jnp.where(live_mask, scores, -1e30)
    peak_score = jnp.maximum(jnp.max(masked, axis=-1), own_score)
    weights = jnp.where(live_mask, jnp.exp(masked - peak_score[..., None]), 0.0)
    own_weight = jnp.exp(own_score - peak_score)
    totals = jnp.sum(weights, axis=-1) + own_weight
    rounded = weights.astype(jnp.bfloat16)
    own_rounded = own_weight.astype(jnp.bfloat16).astype(jnp.float32)
    blended = jnp.einsum(
        "rhgc,rchd->rhgd", rounded, value_blocks, preferred_element_type=jnp.float32
    )
    blended = blended + own_rounded[..., None] * new_value.astype(jnp.float32)[:, :, None, :]
    return (
        (blended / totals[..., None])
        .reshape(row_count, head_count * head_size)
        .astype(jnp.bfloat16)
    )


def shards(
    hidden_rows, query_weight, key_value_weight, cache_keys, earlier_values, lengths, positions
):
    wide_count = lax.axis_size("wide")
    narrow_count = lax.axis_size("narrow")
    query_cols = query_weight.shape[1]
    gathered = lax.all_gather(hidden_rows, "wide", axis=0, tiled=True)
    widened = gathered.astype(jnp.float32)
    squares = lax.psum(jnp.sum(widened * widened, axis=1), "narrow")
    normed = (widened * lax.rsqrt(squares / MODEL_WIDTH + EPSILON)[:, None]).astype(jnp.bfloat16)
    query_part = jnp.dot(normed, query_weight, preferred_element_type=jnp.float32)
    pair_part = jnp.dot(normed, key_value_weight, preferred_element_type=jnp.float32)
    row_each = query_part.shape[0] // (wide_count * narrow_count)
    shaped_query = query_part.reshape(wide_count, narrow_count, row_each, 1, query_cols)
    shaped_pair = pair_part.reshape(
        wide_count, narrow_count, row_each, 1, key_value_weight.shape[1]
    )
    summed_query, summed_pair = (
        lax.psum_scatter(shaped_query, "narrow", scatter_dimension=1, tiled=True),
        lax.psum_scatter(shaped_pair, "narrow", scatter_dimension=1, tiled=True),
    )
    moved_query, moved_pair = (
        lax.all_to_all(
            summed_query.astype(jnp.bfloat16), "wide", split_axis=0, concat_axis=3, tiled=True
        ),
        lax.all_to_all(
            summed_pair.astype(jnp.bfloat16), "wide", split_axis=0, concat_axis=3, tiled=True
        ),
    )
    queries = moved_query.reshape(row_each, -1, HEAD_WIDTH)
    new_pair = moved_pair.reshape(row_each, -1)
    return attend(queries, new_pair, cache_keys, earlier_values, lengths, positions)


WIDE = 8
GROUP = 16
HEADS = GROUP + 2
CHUNKS = 4
ROWS = 4
SLOTS = 192
PACK = 80
MESH = pl.DeviceIdType.MESH


def kernel(
    x_ref, wq_ref, wkv_ref, keys_ref, values_ref, lengths_ref, positions_ref, freq_ref, out_ref,
    gathered, wq, wkv, keys, values, left, acc, give, take, spread, parcel, landed, sums,
    sum_send, sum_recv, own_send, fwd_send, gather_recv, wq_sem, wkv_sem, key_sem, value_sem,
    give_send, give_recv, parcel_send, parcel_recv,
):
    me = lax.axis_index("wide")
    core = lax.axis_index("narrow")
    other = 1 - core
    peer = me + 1 - 2 * lax.rem(me, 2)
    features = x_ref.shape[1]
    width = features // CHUNKS
    half = width // 2

    def wq_copy(c):
        return pltpu.make_async_copy(wq_ref.at[pl.ds(c * width, width)], wq.at[c], wq_sem.at[c])

    def wkv_copy(c):
        return pltpu.make_async_copy(wkv_ref.at[pl.ds(c * width, width)], wkv.at[c], wkv_sem.at[c])

    key_copy = pltpu.make_async_copy(keys_ref, keys, key_sem)
    value_copy = pltpu.make_async_copy(values_ref, values, value_sem)

    barrier = pltpu.get_barrier_semaphore()
    for d in range(1, WIDE):
        pl.semaphore_signal(
            barrier, inc=1, device_id={"wide": lax.rem(me + d, WIDE)}, device_id_type=MESH
        )
    pl.semaphore_signal(barrier, inc=1, device_id={"narrow": other}, device_id_type=MESH)

    for c in range(CHUNKS):
        wq_copy(c).start()
        wkv_copy(c).start()
    key_copy.start()
    value_copy.start()

    widened = x_ref[...].astype(jnp.float32)
    mine = jnp.sum(widened * widened, axis=1, keepdims=True)
    sums[0] = jnp.broadcast_to(mine, (8, 128))
    pl.semaphore_wait(barrier, WIDE)
    swap = pltpu.make_async_remote_copy(
        src_ref=sums.at[0], dst_ref=sums.at[1], send_sem=sum_send, recv_sem=sum_recv,
        device_id={"narrow": other}, device_id_type=MESH,
    )
    swap.start()
    swap.wait()
    squares = sums[0] + sums[1]
    scale = lax.rsqrt(squares / MODEL_WIDTH + EPSILON)[:, :1]

    def send(c, slot, target, sem):
        return pltpu.make_async_remote_copy(
            src_ref=gathered.at[c, slot], dst_ref=gathered.at[c, slot], send_sem=sem,
            recv_sem=gather_recv.at[c, slot], device_id={"wide": target}, device_id_type=MESH,
        )

    def along(c, d):
        return send(c, me, lax.rem(me + 2 * d, WIDE), own_send.at[c, d])

    def across(c):
        return send(c, me, peer, own_send.at[c, 0])

    def forward(c, d):
        return send(c, lax.rem(me + 2 * d, WIDE), peer, fwd_send.at[c, d])

    for c in range(CHUNKS):
        first = x_ref[:, c * width : c * width + half].astype(jnp.float32) * scale
        second = x_ref[:, c * width + half : (c + 1) * width].astype(jnp.float32) * scale
        gathered[c, me] = jnp.concatenate([first, second], axis=0).astype(jnp.bfloat16)
        for d in range(1, 4):
            along(c, d).start()
        across(c).start()

    angles = [positions_ref[r].astype(jnp.float32) * freq_ref[0:1, :] for r in range(ROWS)]
    cosine = [jnp.cos(a) for a in angles]
    sign = jnp.where(lax.broadcasted_iota(jnp.int32, (1, HEAD_WIDTH), 1) < HEAD_WIDTH // 2, -1.0, 1.0)
    sine = [jnp.sin(a) * sign for a in angles]

    def pass_on(c):
        for d in (1, 3, 2):
            slot = lax.rem(me + 2 * d, WIDE)
            send(c, slot, peer, fwd_send.at[c, d]).wait_recv()
            forward(c, d).start()

    pass_on(0)
    for c in range(CHUNKS):
        if c + 1 < CHUNKS:
            pass_on(c + 1)
        for d in range(4):
            slot = lax.rem(peer + 2 * d, WIDE)
            send(c, slot, peer, fwd_send.at[c, 0]).wait_recv()
        block = gathered[c].astype(jnp.float32)
        left[:, :half] = block[:, :8].reshape(8 * WIDE, half).astype(jnp.bfloat16)
        left[:, half:] = block[:, 8:].reshape(8 * WIDE, half).astype(jnp.bfloat16)
        wq_copy(c).wait()
        wkv_copy(c).wait()

        def accumulate(j, product):
            for i in range(2):
                at = pl.ds(pl.multiple_of((2 * j + i) * 64, 64), 64)
                piece = product[:, i * 128 : (i + 1) * 128]
                if c == 0:
                    acc[at, :] = piece
                else:
                    acc[at, :] += piece

        def tile(j, carry):
            columns = pl.ds(pl.multiple_of(j * 256, 256), 256)
            accumulate(
                j, jnp.dot(left[...], wq[c, :, columns], preferred_element_type=jnp.float32)
            )
            return carry

        lax.fori_loop(0, GROUP // 2, tile, 0)
        accumulate(
            GROUP // 2, jnp.dot(left[...], wkv[c], preferred_element_type=jnp.float32)
        )

    for h in range(HEADS):
        for r in range(ROWS):
            give[pl.ds(h * 32 + r * 8, 8), :] = acc[pl.ds(h * 64 + other * 4 + r, 8, stride=8), :]
    trade = pltpu.make_async_remote_copy(
        src_ref=give, dst_ref=take, send_sem=give_send, recv_sem=give_recv,
        device_id={"narrow": other}, device_id_type=MESH,
    )
    trade.start()
    for w in range(WIDE):
        spread[pl.ds(w * PACK + 72, 8), :] = jnp.zeros((8, HEAD_WIDTH), jnp.float32)
    trade.wait()
    for h in range(HEADS):
        for r in range(ROWS):
            total = (
                acc[pl.ds(h * 64 + core * 4 + r, 8, stride=8), :]
                + take[pl.ds(h * 32 + r * 8, 8), :]
            )
            row = r * GROUP + h if h < GROUP else 64 + 2 * r + h - GROUP
            spread[pl.ds(row, 8, stride=PACK), :] = total

    def deliver(d):
        target = lax.rem(me + d, WIDE)
        return pltpu.make_async_remote_copy(
            src_ref=parcel.at[target], dst_ref=landed.at[me], send_sem=parcel_send.at[target],
            recv_sem=parcel_recv.at[me], device_id={"wide": target}, device_id_type=MESH,
        )

    parcel[...] = spread[...].astype(jnp.bfloat16).reshape(WIDE, PACK, HEAD_WIDTH)
    for d in (4, 3, 5, 2, 6, 1, 7):
        deliver(d).start()
    landed[me] = parcel[me]
    key_copy.wait()
    value_copy.wait()
    for d in range(1, WIDE):
        source = lax.rem(me + d, WIDE)
        pltpu.make_async_remote_copy(
            src_ref=parcel.at[source], dst_ref=landed.at[source], send_sem=parcel_send.at[source],
            recv_sem=parcel_recv.at[source], device_id={"wide": source}, device_id_type=MESH,
        ).wait_recv()

    scaling = HEAD_WIDTH ** (-0.5)
    slot_index = lax.broadcasted_iota(jnp.int32, (GROUP, SLOTS), 1)

    def rotated(v, r):
        return (v * cosine[r] + pltpu.roll(v, HEAD_WIDTH // 2, 1) * sine[r]).astype(jnp.bfloat16)

    for r in range(ROWS):
        live = slot_index < lengths_ref[r]
        for g in range(WIDE):
            columns = slice(g * HEAD_WIDTH, (g + 1) * HEAD_WIDTH)
            query = rotated(landed[g, r * GROUP : (r + 1) * GROUP, :].astype(jnp.float32), r)
            pair = landed[g, 64:PACK, :].astype(jnp.float32)
            new_key = rotated(pair, r)[2 * r : 2 * r + 1].astype(jnp.float32)
            new_value = pair[2 * r + 1 : 2 * r + 2]
            own = jnp.sum(query.astype(jnp.float32) * new_key, axis=1, keepdims=True) * scaling
            scores = lax.dot_general(
                query, keys[r, :, columns], (((1,), (1,)), ((), ())),
                preferred_element_type=jnp.float32,
            ) * scaling
            masked = jnp.where(live, scores, -1e30)
            peak = jnp.maximum(jnp.max(masked, axis=1, keepdims=True), own)
            weights = jnp.where(live, jnp.exp(masked - peak), 0.0)
            own_weight = jnp.exp(own - peak)
            totals = jnp.sum(weights, axis=1, keepdims=True) + own_weight
            blended = jnp.dot(
                weights.astype(jnp.bfloat16), values[r, :, columns],
                preferred_element_type=jnp.float32,
            )
            blended = blended + own_weight.astype(jnp.bfloat16).astype(jnp.float32) * new_value
            at = r * WIDE * GROUP + g * GROUP
            out_ref[at : at + GROUP, :] = (blended / totals).astype(jnp.bfloat16)

    for c in range(CHUNKS):
        for d in range(1, 4):
            along(c, d).wait_send()
            forward(c, d).wait_send()
        across(c).wait_send()
    for d in range(1, WIDE):
        deliver(d).wait_send()


def fused(
    hidden_rows, query_weight, key_value_weight, cache_keys, earlier_values, lengths, positions
):
    features = hidden_rows.shape[1]
    width = features // CHUNKS
    frequency = 500000.0 ** (-(jnp.arange(HEAD_WIDTH // 2).astype(jnp.float32) * 2.0 / HEAD_WIDTH))
    frequency = jnp.broadcast_to(jnp.concatenate([frequency, frequency])[None], (8, HEAD_WIDTH))
    dma = pltpu.SemaphoreType.DMA
    vmem, anywhere, smem = (pl.BlockSpec(memory_space=s) for s in (pltpu.VMEM, pl.ANY, pltpu.SMEM))
    result = pl.pallas_call(
        kernel,
        out_shape=jax.ShapeDtypeStruct((ROWS * WIDE * GROUP, HEAD_WIDTH), jnp.bfloat16),
        in_specs=[vmem, anywhere, anywhere, anywhere, anywhere, smem, smem, vmem],
        out_specs=vmem,
        scratch_shapes=[
            pltpu.VMEM((CHUNKS, WIDE, 16, width // 2), jnp.bfloat16),
            pltpu.VMEM((CHUNKS, width, GROUP * HEAD_WIDTH), jnp.bfloat16),
            pltpu.VMEM((CHUNKS, width, 2 * HEAD_WIDTH), jnp.bfloat16),
            pltpu.VMEM((ROWS, SLOTS, WIDE * HEAD_WIDTH), jnp.bfloat16),
            pltpu.VMEM((ROWS, SLOTS, WIDE * HEAD_WIDTH), jnp.bfloat16),
            pltpu.VMEM((8 * WIDE, width), jnp.bfloat16),
            pltpu.VMEM((HEADS * 64, HEAD_WIDTH), jnp.float32),
            pltpu.VMEM((HEADS * 32, HEAD_WIDTH), jnp.float32),
            pltpu.VMEM((HEADS * 32, HEAD_WIDTH), jnp.float32),
            pltpu.VMEM((WIDE * PACK, HEAD_WIDTH), jnp.float32),
            pltpu.VMEM((WIDE, PACK, HEAD_WIDTH), jnp.bfloat16),
            pltpu.VMEM((WIDE, PACK, HEAD_WIDTH), jnp.bfloat16),
            pltpu.VMEM((2, 8, 128), jnp.float32),
            dma, dma, dma((CHUNKS, 4)), dma((CHUNKS, 4)), dma((CHUNKS, WIDE)),
            dma((CHUNKS,)), dma((CHUNKS,)), dma, dma,
            dma, dma, dma((WIDE,)), dma((WIDE,)),
        ],
        compiler_params=pltpu.CompilerParams(
            collective_id=0, has_side_effects=True, vmem_limit_bytes=56 * 1024 * 1024
        ),
    )(
        hidden_rows, query_weight, key_value_weight, cache_keys, earlier_values, lengths,
        positions, frequency,
    )
    return result.reshape(ROWS, WIDE * GROUP * HEAD_WIDTH)


def solution(mesh):
    body = fused if mesh.shape["wide"] == WIDE and mesh.shape["narrow"] == 2 else shards
    in_specs = (
        P(("rep", "wide"), "narrow"),
        P("narrow", "wide"),
        P("narrow", "wide"),
        P(("rep", "wide", "narrow"), None, None),
        P(("rep", "wide", "narrow"), None, None),
        P(("rep", "wide", "narrow")),
        P(("rep", "wide", "narrow")),
    )
    out_specs = P(("rep", "wide", "narrow"), None)
    return jax.shard_map(body, mesh=mesh, in_specs=in_specs, out_specs=out_specs, check_vma=False)
```

```python
import functools

import jax
import jax.numpy as jnp
import numpy as np
from jax import lax
from jax.experimental import pallas as pl
from jax.experimental.pallas import tpu as pltpu
from jax.sharding import PartitionSpec as P

MODEL_WIDTH = 16384
HEAD_WIDTH = 128


EPSILON = 1e-05


def rotate(values, positions):
    middle = values.shape[-1] // 2
    frequency = 500000.0 ** (-(jnp.arange(middle).astype(jnp.float32) * 2.0 / values.shape[-1]))
    angles = positions.astype(jnp.float32)[:, None] * frequency[None, :]
    cosine = jnp.cos(angles)[:, None, :]
    sine_part = jnp.sin(angles)[:, None, :]
    leading = values[..., :middle]
    trailing = values[..., middle:]
    return jnp.concatenate(
        [leading * cosine - trailing * sine_part, trailing * cosine + leading * sine_part], axis=-1
    )


def attend(queries, new_pair, cached_keys, cached_values, lengths, positions):
    row_count, head_count, head_size = queries.shape
    kv_heads = cached_keys.shape[-1] // head_size
    group_size = head_count // kv_heads
    rotated = rotate(queries.astype(jnp.float32), positions).astype(jnp.bfloat16)
    split_pair = new_pair.reshape(row_count, kv_heads, 2, head_size)
    new_key = rotate(split_pair[:, :, 0, :].astype(jnp.float32), positions).astype(jnp.bfloat16)
    new_value = split_pair[:, :, 1, :]
    grouped = rotated.reshape(row_count, kv_heads, group_size, head_size)
    key_blocks = cached_keys.reshape(row_count, -1, kv_heads, head_size)
    value_blocks = cached_values.reshape(row_count, -1, kv_heads, head_size)
    scaling = head_size ** (-0.5)
    scores = (
        jnp.einsum("rhgd,rchd->rhgc", grouped, key_blocks, preferred_element_type=jnp.float32)
        * scaling
    )
    own_score = (
        jnp.einsum("rhgd,rhd->rhg", grouped, new_key, preferred_element_type=jnp.float32) * scaling
    )
    live_mask = (jnp.arange(key_blocks.shape[1])[None, :] < lengths[:, None])[:, None, None, :]
    masked = jnp.where(live_mask, scores, -1e30)
    peak_score = jnp.maximum(jnp.max(masked, axis=-1), own_score)
    weights = jnp.where(live_mask, jnp.exp(masked - peak_score[..., None]), 0.0)
    own_weight = jnp.exp(own_score - peak_score)
    totals = jnp.sum(weights, axis=-1) + own_weight
    rounded = weights.astype(jnp.bfloat16)
    own_rounded = own_weight.astype(jnp.bfloat16).astype(jnp.float32)
    blended = jnp.einsum(
        "rhgc,rchd->rhgd", rounded, value_blocks, preferred_element_type=jnp.float32
    )
    blended = blended + own_rounded[..., None] * new_value.astype(jnp.float32)[:, :, None, :]
    return (
        (blended / totals[..., None])
        .reshape(row_count, head_count * head_size)
        .astype(jnp.bfloat16)
    )


def shards(
    hidden_rows, query_weight, key_value_weight, cache_keys, earlier_values, lengths, positions
):
    wide_count = lax.axis_size("wide")
    narrow_count = lax.axis_size("narrow")
    query_cols = query_weight.shape[1]
    gathered = lax.all_gather(hidden_rows, "wide", axis=0, tiled=True)
    widened = gathered.astype(jnp.float32)
    squares = lax.psum(jnp.sum(widened * widened, axis=1), "narrow")
    normed = (widened * lax.rsqrt(squares / MODEL_WIDTH + EPSILON)[:, None]).astype(jnp.bfloat16)
    query_part = jnp.dot(normed, query_weight, preferred_element_type=jnp.float32)
    pair_part = jnp.dot(normed, key_value_weight, preferred_element_type=jnp.float32)
    row_each = query_part.shape[0] // (wide_count * narrow_count)
    shaped_query = query_part.reshape(wide_count, narrow_count, row_each, 1, query_cols)
    shaped_pair = pair_part.reshape(
        wide_count, narrow_count, row_each, 1, key_value_weight.shape[1]
    )
    summed_query, summed_pair = (
        lax.psum_scatter(shaped_query, "narrow", scatter_dimension=1, tiled=True),
        lax.psum_scatter(shaped_pair, "narrow", scatter_dimension=1, tiled=True),
    )
    moved_query, moved_pair = (
        lax.all_to_all(
            summed_query.astype(jnp.bfloat16), "wide", split_axis=0, concat_axis=3, tiled=True
        ),
        lax.all_to_all(
            summed_pair.astype(jnp.bfloat16), "wide", split_axis=0, concat_axis=3, tiled=True
        ),
    )
    queries = moved_query.reshape(row_each, -1, HEAD_WIDTH)
    new_pair = moved_pair.reshape(row_each, -1)
    return attend(queries, new_pair, cache_keys, earlier_values, lengths, positions)


WIDE = 8
GROUP = 16
HEADS = GROUP + 2
CUTS = (0, 8, 16, 24, 32)
CHUNKS = len(CUTS) - 1
TILE = 512
ROWS = 4
SLOTS = 192
PACK = 80
MESH = pl.DeviceIdType.MESH


def kernel(
    x_ref, wq_ref, wkv_ref, keys_ref, values_ref, lengths_ref, positions_ref, out_ref,
    gathered, wq, wkv, keys, values, left, acc, give, take, spread, parcel, landed, sums,
    sum_send, sum_recv, own_send, across_send, gather_recv, weight_sem, key_sem, value_sem,
    give_send, give_recv, parcel_send, parcel_recv,
):
    me = lax.axis_index("wide")
    core = lax.axis_index("narrow")
    other = 1 - core
    peer = me + 1 - 2 * lax.rem(me, 2)
    features = x_ref.shape[1]
    half = features // 2
    cuts = [half // CUTS[-1] * cut for cut in CUTS]

    def span(c):
        return pl.ds(cuts[c], cuts[c + 1] - cuts[c])

    def lower(c):
        return pl.ds(half + cuts[c], cuts[c + 1] - cuts[c])

    def weight_copies(c):
        return [
            pltpu.make_async_copy(source.at[rows], kept.at[rows], weight_sem.at[c, i, j])
            for i, (source, kept) in enumerate(((wq_ref, wq), (wkv_ref, wkv)))
            for j, rows in enumerate((span(c), lower(c)))
        ]

    key_copy = pltpu.make_async_copy(keys_ref, keys, key_sem)
    value_copy = pltpu.make_async_copy(values_ref, values, value_sem)

    barrier = pltpu.get_barrier_semaphore()
    for d in range(1, WIDE):
        pl.semaphore_signal(
            barrier, inc=1, device_id={"wide": lax.rem(me + d, WIDE)}, device_id_type=MESH
        )
    pl.semaphore_signal(barrier, inc=1, device_id={"narrow": other}, device_id_type=MESH)

    for c in range(CHUNKS):
        for copy in weight_copies(c):
            copy.start()
    key_copy.start()
    value_copy.start()

    widened = x_ref[...].astype(jnp.float32)
    mine = jnp.sum(widened * widened, axis=1, keepdims=True)
    sums[0] = jnp.broadcast_to(mine, (8, 128))
    pl.semaphore_wait(barrier, WIDE)
    swap = pltpu.make_async_remote_copy(
        src_ref=sums.at[0], dst_ref=sums.at[1], send_sem=sum_send, recv_sem=sum_recv,
        device_id={"narrow": other}, device_id_type=MESH,
    )
    swap.start()
    swap.wait()
    squares = sums[0] + sums[1]
    scale = lax.rsqrt(squares / MODEL_WIDTH + EPSILON)[:, :1]

    def send(c, slot, target, sem):
        return pltpu.make_async_remote_copy(
            src_ref=gathered.at[slot, :, span(c)], dst_ref=gathered.at[slot, :, span(c)], send_sem=sem,
            recv_sem=gather_recv.at[c, slot], device_id={"wide": target}, device_id_type=MESH,
        )

    def across(c, slot):
        return send(c, slot, peer, across_send.at[c, slot])

    def along(c, d):
        return send(c, me, lax.rem(me + 2 * d, WIDE), own_send.at[c, d])

    def relay(c, d):
        slot = lax.rem(me + 2 * d, WIDE)
        across(c, slot).wait_recv()
        across(c, slot).start()

    def originate(c):
        first = x_ref[:, span(c)].astype(jnp.float32) * scale
        second = x_ref[:, lower(c)].astype(jnp.float32) * scale
        gathered[me, :, span(c)] = jnp.concatenate([first, second], axis=0).astype(jnp.bfloat16)
        for d in range(1, 4):
            along(c, d).start()
        across(c, me).start()

    def multiply(c, between):
        for level_at in range(WIDE // 2):
            across(c, 2 * level_at + lax.rem(peer, 2)).wait_recv()
        block = gathered[:, :, span(c)].astype(jnp.float32)
        size = cuts[c + 1] - cuts[c]
        left[:, span(c)] = block[:, :8].reshape(8 * WIDE, size).astype(jnp.bfloat16)
        left[:, lower(c)] = block[:, 8:].reshape(8 * WIDE, size).astype(jnp.bfloat16)
        for copy in weight_copies(c):
            copy.wait()

        def accumulate(start, columns, kept):
            product = jnp.dot(
                left[:, span(c)], kept[span(c), columns], preferred_element_type=jnp.float32
            ) + jnp.dot(
                left[:, lower(c)], kept[lower(c), columns], preferred_element_type=jnp.float32
            )
            for i in range(product.shape[1] // 128):
                at = pl.ds(start + i * 64, 64)
                piece = product[:, i * 128 : (i + 1) * 128]
                if c == 0:
                    acc[at, :] = piece
                else:
                    acc[at, :] += piece

        tiles = GROUP * HEAD_WIDTH // TILE
        for j in range(tiles):
            accumulate(j * TILE // 2, pl.ds(j * TILE, TILE), wq)
            if j < len(between):
                between[j]()
        for step in between[tiles:]:
            step()
        accumulate(GROUP * 64, pl.ds(0, 2 * HEAD_WIDTH), wkv)

    def ahead(c, d):
        if c < CHUNKS:
            relay(c, d)

    for c in range(CHUNKS):
        originate(c)
    lane = lax.broadcasted_iota(jnp.int32, (1, HEAD_WIDTH), 1)
    frequency = jnp.ones((1, HEAD_WIDTH), jnp.float32)
    for bit in range(6):
        factor = float(np.float32(500000.0 ** (-(2.0**bit) / 64)))
        frequency = frequency * jnp.where((lane // 2**bit) % 2 == 1, factor, 1.0)
    angles = [positions_ref[r].astype(jnp.float32) * frequency for r in range(ROWS)]
    cosine = [jnp.cos(a) for a in angles]
    sign = jnp.where(lane < HEAD_WIDTH // 2, -1.0, 1.0)
    sine = [jnp.sin(a) * sign for a in angles]
    for c in range(2):
        for d in (1, 3, 2):
            relay(c, d)
    for c in range(CHUNKS):
        multiply(c, [functools.partial(ahead, c + 2, d) for d in (1, 3, 2)])

    for h in range(HEADS):
        for r in range(ROWS):
            give[pl.ds(h * 32 + r * 8, 8), :] = acc[pl.ds(h * 64 + other * 4 + r, 8, stride=8), :]
    trade = pltpu.make_async_remote_copy(
        src_ref=give, dst_ref=take, send_sem=give_send, recv_sem=give_recv,
        device_id={"narrow": other}, device_id_type=MESH,
    )
    trade.start()
    for w in range(WIDE):
        spread[pl.ds(w * PACK + 72, 8), :] = jnp.zeros((8, HEAD_WIDTH), jnp.float32)
    trade.wait()
    for h in range(HEADS):
        for r in range(ROWS):
            total = (
                acc[pl.ds(h * 64 + core * 4 + r, 8, stride=8), :]
                + take[pl.ds(h * 32 + r * 8, 8), :]
            )
            row = r * GROUP + h if h < GROUP else 64 + 2 * r + h - GROUP
            spread[pl.ds(row, 8, stride=PACK), :] = total

    def deliver(d):
        target = lax.rem(me + d, WIDE)
        return pltpu.make_async_remote_copy(
            src_ref=parcel.at[target], dst_ref=landed.at[me], send_sem=parcel_send.at[target],
            recv_sem=parcel_recv.at[me], device_id={"wide": target}, device_id_type=MESH,
        )

    parcel[...] = spread[...].astype(jnp.bfloat16).reshape(WIDE, PACK, HEAD_WIDTH)
    for d in (4, 3, 5, 2, 6, 1, 7):
        deliver(d).start()
    landed[me] = parcel[me]
    key_copy.wait()
    value_copy.wait()
    for d in range(1, WIDE):
        source = lax.rem(me + d, WIDE)
        pltpu.make_async_remote_copy(
            src_ref=parcel.at[source], dst_ref=landed.at[source], send_sem=parcel_send.at[source],
            recv_sem=parcel_recv.at[source], device_id={"wide": source}, device_id_type=MESH,
        ).wait_recv()

    scaling = HEAD_WIDTH ** (-0.5)
    slot_index = lax.broadcasted_iota(jnp.int32, (WIDE * GROUP, SLOTS), 1)
    none = jnp.zeros((GROUP, HEAD_WIDTH), jnp.bfloat16)
    pair = landed[:, 64:PACK, :].astype(jnp.float32)

    def rotated(v, r):
        return (v * cosine[r] + pltpu.roll(v, HEAD_WIDTH // 2, 1) * sine[r]).astype(jnp.bfloat16)

    def wide(start):
        return slice(start * 2 * HEAD_WIDTH, (start + 1) * 2 * HEAD_WIDTH)

    queries, owns, new_values, scores = [], [], [], []
    for r in range(ROWS):
        raw = landed[:, r * GROUP : (r + 1) * GROUP, :].astype(jnp.float32)
        query = rotated(raw.reshape(WIDE * GROUP, HEAD_WIDTH), r)
        new_key = pair[:, 2 * r : 2 * r + 1, :].reshape(WIDE, HEAD_WIDTH)
        new_key = rotated(new_key, r).astype(jnp.float32).reshape(WIDE, 1, HEAD_WIDTH)
        grouped = query.astype(jnp.float32).reshape(WIDE, GROUP, HEAD_WIDTH)
        own = jnp.sum(grouped * new_key, axis=2, keepdims=True) * scaling
        owns.append(own.reshape(WIDE * GROUP, 1))
        new_values.append(pair[:, 2 * r + 1 : 2 * r + 2, :])
        parts = []
        for p in range(WIDE // 2):
            even = query[2 * p * GROUP : (2 * p + 1) * GROUP]
            odd = query[(2 * p + 1) * GROUP : (2 * p + 2) * GROUP]
            both = jnp.concatenate(
                [jnp.concatenate([even, none], axis=1), jnp.concatenate([none, odd], axis=1)], axis=0
            )
            parts.append(
                lax.dot_general(
                    both, keys[r, :, wide(p)], (((1,), (1,)), ((), ())),
                    preferred_element_type=jnp.float32,
                )
            )
        scores.append(jnp.concatenate(parts, axis=0) * scaling)
    for r in range(ROWS):
        live = slot_index < lengths_ref[r]
        masked = jnp.where(live, scores[r], -1e30)
        peak = jnp.maximum(jnp.max(masked, axis=1, keepdims=True), owns[r])
        weights = jnp.where(live, jnp.exp(masked - peak), 0.0)
        own_weight = jnp.exp(owns[r] - peak)
        totals = jnp.sum(weights, axis=1, keepdims=True) + own_weight
        rounded = weights.astype(jnp.bfloat16)
        parts = []
        for p in range(WIDE // 2):
            both = jnp.dot(
                rounded[2 * p * GROUP : (2 * p + 2) * GROUP], values[r, :, wide(p)],
                preferred_element_type=jnp.float32,
            )
            parts += [both[:GROUP, :HEAD_WIDTH], both[GROUP:, HEAD_WIDTH:]]
        own_rounded = own_weight.astype(jnp.bfloat16).astype(jnp.float32)
        added = own_rounded.reshape(WIDE, GROUP, 1) * new_values[r]
        blended = jnp.concatenate(parts, axis=0) + added.reshape(WIDE * GROUP, HEAD_WIDTH)
        at = r * WIDE * GROUP
        out_ref[at : at + WIDE * GROUP, :] = (blended * (1.0 / totals)).astype(jnp.bfloat16)

    for c in range(CHUNKS):
        for k in range(WIDE // 2):
            across(c, 2 * k + lax.rem(me, 2)).wait_send()
        for d in range(1, 4):
            along(c, d).wait_send()
    for d in range(1, WIDE):
        deliver(d).wait_send()


def fused(
    hidden_rows, query_weight, key_value_weight, cache_keys, earlier_values, lengths, positions
):
    features = hidden_rows.shape[1]
    dma = pltpu.SemaphoreType.DMA
    vmem, anywhere, smem = (pl.BlockSpec(memory_space=s) for s in (pltpu.VMEM, pl.ANY, pltpu.SMEM))
    result = pl.pallas_call(
        kernel,
        out_shape=jax.ShapeDtypeStruct((ROWS * WIDE * GROUP, HEAD_WIDTH), jnp.bfloat16),
        in_specs=[vmem, anywhere, anywhere, anywhere, anywhere, smem, smem],
        out_specs=vmem,
        scratch_shapes=[
            pltpu.VMEM((WIDE, 16, features // 2), jnp.bfloat16),
            pltpu.VMEM((features, GROUP * HEAD_WIDTH), jnp.bfloat16),
            pltpu.VMEM((features, 2 * HEAD_WIDTH), jnp.bfloat16),
            pltpu.VMEM((ROWS, SLOTS, WIDE * HEAD_WIDTH), jnp.bfloat16),
            pltpu.VMEM((ROWS, SLOTS, WIDE * HEAD_WIDTH), jnp.bfloat16),
            pltpu.VMEM((8 * WIDE, features), jnp.bfloat16),
            pltpu.VMEM((HEADS * 64, HEAD_WIDTH), jnp.float32),
            pltpu.VMEM((HEADS * 32, HEAD_WIDTH), jnp.float32),
            pltpu.VMEM((HEADS * 32, HEAD_WIDTH), jnp.float32),
            pltpu.VMEM((WIDE * PACK, HEAD_WIDTH), jnp.float32),
            pltpu.VMEM((WIDE, PACK, HEAD_WIDTH), jnp.bfloat16),
            pltpu.VMEM((WIDE, PACK, HEAD_WIDTH), jnp.bfloat16),
            pltpu.VMEM((2, 8, 128), jnp.float32),
            dma, dma, dma((CHUNKS, 4)), dma((CHUNKS, WIDE)), dma((CHUNKS, WIDE)),
            dma((CHUNKS, 2, 2)), dma, dma,
            dma, dma, dma((WIDE,)), dma((WIDE,)),
        ],
        compiler_params=pltpu.CompilerParams(
            collective_id=0, has_side_effects=True, vmem_limit_bytes=56 * 1024 * 1024
        ),
    )(
        hidden_rows, query_weight, key_value_weight, cache_keys, earlier_values, lengths,
        positions,
    )
    return result.reshape(ROWS, WIDE * GROUP * HEAD_WIDTH)


def solution(mesh):
    body = fused if mesh.shape["wide"] == WIDE and mesh.shape["narrow"] == 2 else shards
    in_specs = (
        P(("rep", "wide"), "narrow"),
        P("narrow", "wide"),
        P("narrow", "wide"),
        P(("rep", "wide", "narrow"), None, None),
        P(("rep", "wide", "narrow"), None, None),
        P(("rep", "wide", "narrow")),
        P(("rep", "wide", "narrow")),
    )
    out_specs = P(("rep", "wide", "narrow"), None)
    return jax.shard_map(body, mesh=mesh, in_specs=in_specs, out_specs=out_specs, check_vma=False)
```

```python
import functools

import jax
import jax.numpy as jnp
import numpy as np
from jax import lax
from jax.experimental import pallas as pl
from jax.experimental.pallas import tpu as pltpu
from jax.sharding import PartitionSpec as P

MODEL_WIDTH = 16384
HEAD_WIDTH = 128


EPSILON = 1e-05


def rotate(values, positions):
    middle = values.shape[-1] // 2
    frequency = 500000.0 ** (-(jnp.arange(middle).astype(jnp.float32) * 2.0 / values.shape[-1]))
    angles = positions.astype(jnp.float32)[:, None] * frequency[None, :]
    cosine = jnp.cos(angles)[:, None, :]
    sine_part = jnp.sin(angles)[:, None, :]
    leading = values[..., :middle]
    trailing = values[..., middle:]
    return jnp.concatenate(
        [leading * cosine - trailing * sine_part, trailing * cosine + leading * sine_part], axis=-1
    )


def attend(queries, new_pair, cached_keys, cached_values, lengths, positions):
    row_count, head_count, head_size = queries.shape
    kv_heads = cached_keys.shape[-1] // head_size
    group_size = head_count // kv_heads
    rotated = rotate(queries.astype(jnp.float32), positions).astype(jnp.bfloat16)
    split_pair = new_pair.reshape(row_count, kv_heads, 2, head_size)
    new_key = rotate(split_pair[:, :, 0, :].astype(jnp.float32), positions).astype(jnp.bfloat16)
    new_value = split_pair[:, :, 1, :]
    grouped = rotated.reshape(row_count, kv_heads, group_size, head_size)
    key_blocks = cached_keys.reshape(row_count, -1, kv_heads, head_size)
    value_blocks = cached_values.reshape(row_count, -1, kv_heads, head_size)
    scaling = head_size ** (-0.5)
    scores = (
        jnp.einsum("rhgd,rchd->rhgc", grouped, key_blocks, preferred_element_type=jnp.float32)
        * scaling
    )
    own_score = (
        jnp.einsum("rhgd,rhd->rhg", grouped, new_key, preferred_element_type=jnp.float32) * scaling
    )
    live_mask = (jnp.arange(key_blocks.shape[1])[None, :] < lengths[:, None])[:, None, None, :]
    masked = jnp.where(live_mask, scores, -1e30)
    peak_score = jnp.maximum(jnp.max(masked, axis=-1), own_score)
    weights = jnp.where(live_mask, jnp.exp(masked - peak_score[..., None]), 0.0)
    own_weight = jnp.exp(own_score - peak_score)
    totals = jnp.sum(weights, axis=-1) + own_weight
    rounded = weights.astype(jnp.bfloat16)
    own_rounded = own_weight.astype(jnp.bfloat16).astype(jnp.float32)
    blended = jnp.einsum(
        "rhgc,rchd->rhgd", rounded, value_blocks, preferred_element_type=jnp.float32
    )
    blended = blended + own_rounded[..., None] * new_value.astype(jnp.float32)[:, :, None, :]
    return (
        (blended / totals[..., None])
        .reshape(row_count, head_count * head_size)
        .astype(jnp.bfloat16)
    )


def shards(
    hidden_rows, query_weight, key_value_weight, cache_keys, earlier_values, lengths, positions
):
    wide_count = lax.axis_size("wide")
    narrow_count = lax.axis_size("narrow")
    query_cols = query_weight.shape[1]
    gathered = lax.all_gather(hidden_rows, "wide", axis=0, tiled=True)
    widened = gathered.astype(jnp.float32)
    squares = lax.psum(jnp.sum(widened * widened, axis=1), "narrow")
    normed = (widened * lax.rsqrt(squares / MODEL_WIDTH + EPSILON)[:, None]).astype(jnp.bfloat16)
    query_part = jnp.dot(normed, query_weight, preferred_element_type=jnp.float32)
    pair_part = jnp.dot(normed, key_value_weight, preferred_element_type=jnp.float32)
    row_each = query_part.shape[0] // (wide_count * narrow_count)
    shaped_query = query_part.reshape(wide_count, narrow_count, row_each, 1, query_cols)
    shaped_pair = pair_part.reshape(
        wide_count, narrow_count, row_each, 1, key_value_weight.shape[1]
    )
    summed_query, summed_pair = (
        lax.psum_scatter(shaped_query, "narrow", scatter_dimension=1, tiled=True),
        lax.psum_scatter(shaped_pair, "narrow", scatter_dimension=1, tiled=True),
    )
    moved_query, moved_pair = (
        lax.all_to_all(
            summed_query.astype(jnp.bfloat16), "wide", split_axis=0, concat_axis=3, tiled=True
        ),
        lax.all_to_all(
            summed_pair.astype(jnp.bfloat16), "wide", split_axis=0, concat_axis=3, tiled=True
        ),
    )
    queries = moved_query.reshape(row_each, -1, HEAD_WIDTH)
    new_pair = moved_pair.reshape(row_each, -1)
    return attend(queries, new_pair, cache_keys, earlier_values, lengths, positions)


WIDE = 8
GROUP = 16
HEADS = GROUP + 2
CUTS = (0, 8, 16, 24, 32)
CHUNKS = len(CUTS) - 1
TILE = 512
ROWS = 4
SLOTS = 192
PACK = 80
PARTS = ((0, 32), (32, PACK))
HALVES = ((0, 8), (8, HEADS))
MESH = pl.DeviceIdType.MESH


def kernel(
    x_ref, wq_ref, wkv_ref, keys_ref, values_ref, lengths_ref, positions_ref, out_ref,
    gathered, wq, wkv, keys, values, left, acc, give, take, spread, parcel, landed, sums, final,
    sum_send, sum_recv, own_send, across_send, gather_recv, weight_sem, key_sem, value_sem,
    give_send, give_recv, parcel_send, parcel_recv,
):
    me = lax.axis_index("wide")
    core = lax.axis_index("narrow")
    other = 1 - core
    peer = me + 1 - 2 * lax.rem(me, 2)
    features = x_ref.shape[1]
    half = features // 2
    cuts = [half // CUTS[-1] * cut for cut in CUTS]

    def span(c):
        return pl.ds(cuts[c], cuts[c + 1] - cuts[c])

    def lower(c):
        return pl.ds(half + cuts[c], cuts[c + 1] - cuts[c])

    def weight_copies(c):
        return [
            pltpu.make_async_copy(source.at[rows], kept.at[rows], weight_sem.at[c, i, j])
            for i, (source, kept) in enumerate(((wq_ref, wq), (wkv_ref, wkv)))
            for j, rows in enumerate((span(c), lower(c)))
        ]

    key_copy = pltpu.make_async_copy(keys_ref, keys, key_sem)
    value_copy = pltpu.make_async_copy(values_ref, values, value_sem)

    barrier = pltpu.get_barrier_semaphore()
    for d in range(1, WIDE):
        pl.semaphore_signal(
            barrier, inc=1, device_id={"wide": lax.rem(me + d, WIDE)}, device_id_type=MESH
        )
    pl.semaphore_signal(barrier, inc=1, device_id={"narrow": other}, device_id_type=MESH)

    for c in range(CHUNKS):
        for copy in weight_copies(c):
            copy.start()
    key_copy.start()
    value_copy.start()

    widened = x_ref[...].astype(jnp.float32)
    mine = jnp.sum(widened * widened, axis=1, keepdims=True)
    sums[0] = jnp.broadcast_to(mine, (8, 128))
    pl.semaphore_wait(barrier, WIDE)
    swap = pltpu.make_async_remote_copy(
        src_ref=sums.at[0], dst_ref=sums.at[1], send_sem=sum_send, recv_sem=sum_recv,
        device_id={"narrow": other}, device_id_type=MESH,
    )
    swap.start()
    swap.wait()
    squares = sums[0] + sums[1]
    scale = lax.rsqrt(squares / MODEL_WIDTH + EPSILON)[:, :1]

    def send(c, slot, target, sem):
        return pltpu.make_async_remote_copy(
            src_ref=gathered.at[slot, :, span(c)], dst_ref=gathered.at[slot, :, span(c)], send_sem=sem,
            recv_sem=gather_recv.at[c, slot], device_id={"wide": target}, device_id_type=MESH,
        )

    def across(c, slot):
        return send(c, slot, peer, across_send.at[c, slot])

    def along(c, d):
        return send(c, me, lax.rem(me + 2 * d, WIDE), own_send.at[c, d])

    def relay(c, d):
        slot = lax.rem(me + 2 * d, WIDE)
        across(c, slot).wait_recv()
        across(c, slot).start()

    def originate(c):
        first = x_ref[:, span(c)].astype(jnp.float32) * scale
        second = x_ref[:, lower(c)].astype(jnp.float32) * scale
        gathered[me, :, span(c)] = jnp.concatenate([first, second], axis=0).astype(jnp.bfloat16)
        for d in range(1, 4):
            along(c, d).start()
        across(c, me).start()

    def multiply(c, between):
        for level_at in range(WIDE // 2):
            across(c, 2 * level_at + lax.rem(peer, 2)).wait_recv()
        block = gathered[:, :, span(c)].astype(jnp.float32)
        size = cuts[c + 1] - cuts[c]
        left[:, span(c)] = block[:, :8].reshape(8 * WIDE, size).astype(jnp.bfloat16)
        left[:, lower(c)] = block[:, 8:].reshape(8 * WIDE, size).astype(jnp.bfloat16)
        for copy in weight_copies(c):
            copy.wait()

        def accumulate(start, columns, kept):
            product = jnp.dot(
                left[:, span(c)], kept[span(c), columns], preferred_element_type=jnp.float32
            ) + jnp.dot(
                left[:, lower(c)], kept[lower(c), columns], preferred_element_type=jnp.float32
            )
            for i in range(product.shape[1] // 128):
                at = pl.ds(start + i * 64, 64)
                piece = product[:, i * 128 : (i + 1) * 128]
                if c == 0:
                    acc[at, :] = piece
                else:
                    acc[at, :] += piece

        tiles = GROUP * HEAD_WIDTH // TILE
        for j in range(tiles):
            accumulate(j * TILE // 2, pl.ds(j * TILE, TILE), wq)
            if j < len(between):
                between[j]()
        for step in between[tiles:]:
            step()
        accumulate(GROUP * 64, pl.ds(0, 2 * HEAD_WIDTH), wkv)

    def ahead(c, d):
        if c < CHUNKS:
            relay(c, d)

    for c in range(CHUNKS):
        originate(c)
    lane = lax.broadcasted_iota(jnp.int32, (1, HEAD_WIDTH), 1)
    frequency = jnp.ones((1, HEAD_WIDTH), jnp.float32)
    for bit in range(6):
        factor = float(np.float32(500000.0 ** (-(2.0**bit) / 64)))
        frequency = frequency * jnp.where((lane // 2**bit) % 2 == 1, factor, 1.0)
    angles = [positions_ref[r].astype(jnp.float32) * frequency for r in range(ROWS)]
    cosine = [jnp.cos(a) for a in angles]
    sign = jnp.where(lane < HEAD_WIDTH // 2, -1.0, 1.0)
    sine = [jnp.sin(a) * sign for a in angles]
    for c in range(2):
        for d in (1, 3, 2):
            relay(c, d)
    def trade(p):
        rows = pl.ds(HALVES[p][0] * 32, (HALVES[p][1] - HALVES[p][0]) * 32)
        return pltpu.make_async_remote_copy(
            src_ref=give.at[rows], dst_ref=take.at[rows], send_sem=give_send.at[p],
            recv_sem=give_recv.at[p], device_id={"narrow": other}, device_id_type=MESH,
        )

    def offer(p):
        for h in range(*HALVES[p]):
            for r in range(ROWS):
                kept = acc[pl.ds(h * 64 + other * 4 + r, 8, stride=8), :]
                give[pl.ds(h * 32 + r * 8, 8), :] = kept
        trade(p).start()

    def deliver(d, p, slot):
        target = lax.rem(me + d, WIDE)
        rows = pl.ds(PARTS[p][0], PARTS[p][1] - PARTS[p][0])
        return pltpu.make_async_remote_copy(
            src_ref=parcel.at[target, rows], dst_ref=landed.at[slot, rows],
            send_sem=parcel_send.at[target, p], recv_sem=parcel_recv.at[slot, p],
            device_id={"wide": target}, device_id_type=MESH,
        )

    def dispatch(p):
        trade(p).wait()
        start, stop = PARTS[p]
        for h in range(*HALVES[p]):
            for r in range(ROWS):
                total = (
                    acc[pl.ds(h * 64 + core * 4 + r, 8, stride=8), :]
                    + take[pl.ds(h * 32 + r * 8, 8), :]
                )
                row = h // 8 * 32 + r * 8 + h % 8 if h < GROUP else 64 + 2 * r + h - GROUP
                spread[pl.ds(row, 8, stride=PACK), :] = total
        for w in range(WIDE):
            parcel[w, start:stop, :] = spread[w * PACK + start : w * PACK + stop, :].astype(
                jnp.bfloat16
            )
        for d in (4, 3, 5, 2, 6, 1, 7):
            deliver(d, p, me).start()
        landed[me, start:stop, :] = parcel[me, start:stop, :]

    for w in range(WIDE):
        spread[pl.ds(w * PACK + 72, 8), :] = jnp.zeros((8, HEAD_WIDTH), jnp.float32)
    for c in range(CHUNKS - 1):
        multiply(c, [functools.partial(ahead, c + 2, d) for d in (1, 3, 2)])
    multiply(CHUNKS - 1, [lambda: None, lambda: offer(0), lambda: None, lambda: dispatch(0)])
    offer(1)
    dispatch(1)
    key_copy.wait()
    value_copy.wait()
    for p in range(2):
        for d in range(1, WIDE):
            deliver(d, p, lax.rem(me + d, WIDE)).wait_recv()

    scaling = HEAD_WIDTH ** (-0.5)
    slot_index = lax.broadcasted_iota(jnp.int32, (WIDE * GROUP, SLOTS), 1)
    none = jnp.zeros((GROUP, HEAD_WIDTH), jnp.bfloat16)
    pair = landed[:, 64:PACK, :].astype(jnp.float32)
    early = landed[:, :32, :].astype(jnp.float32)
    later = landed[:, 32:64, :].astype(jnp.float32)

    def rotated(v, r):
        return (v * cosine[r] + pltpu.roll(v, HEAD_WIDTH // 2, 1) * sine[r]).astype(jnp.bfloat16)

    def wide(start):
        return slice(start * 2 * HEAD_WIDTH, (start + 1) * 2 * HEAD_WIDTH)

    queries, owns, new_values, scores = [], [], [], []
    for r in range(ROWS):
        raw = jnp.concatenate(
            [early[:, r * 8 : (r + 1) * 8, :], later[:, r * 8 : (r + 1) * 8, :]], axis=1
        )
        query = rotated(raw.reshape(WIDE * GROUP, HEAD_WIDTH), r)
        new_key = pair[:, 2 * r : 2 * r + 1, :].reshape(WIDE, HEAD_WIDTH)
        new_key = rotated(new_key, r).astype(jnp.float32).reshape(WIDE, 1, HEAD_WIDTH)
        grouped = query.astype(jnp.float32).reshape(WIDE, GROUP, HEAD_WIDTH)
        own = jnp.sum(grouped * new_key, axis=2, keepdims=True) * scaling
        owns.append(own.reshape(WIDE * GROUP, 1))
        new_values.append(pair[:, 2 * r + 1 : 2 * r + 2, :])
        parts = []
        for p in range(WIDE // 2):
            even = query[2 * p * GROUP : (2 * p + 1) * GROUP]
            odd = query[(2 * p + 1) * GROUP : (2 * p + 2) * GROUP]
            both = jnp.concatenate(
                [jnp.concatenate([even, none], axis=1), jnp.concatenate([none, odd], axis=1)], axis=0
            )
            parts.append(
                lax.dot_general(
                    both, keys[r, :, wide(p)], (((1,), (1,)), ((), ())),
                    preferred_element_type=jnp.float32,
                )
            )
        scores.append(jnp.concatenate(parts, axis=0) * scaling)
    for r in range(ROWS):
        live = slot_index < lengths_ref[r]
        masked = jnp.where(live, scores[r], -1e30)
        peak = jnp.maximum(jnp.max(masked, axis=1, keepdims=True), owns[r])
        weights = jnp.where(live, jnp.exp(masked - peak), 0.0)
        own_weight = jnp.exp(owns[r] - peak)
        totals = jnp.sum(weights, axis=1, keepdims=True) + own_weight
        rounded = weights.astype(jnp.bfloat16)
        parts = []
        for p in range(WIDE // 2):
            both = jnp.dot(
                rounded[2 * p * GROUP : (2 * p + 2) * GROUP], values[r, :, wide(p)],
                preferred_element_type=jnp.float32,
            )
            parts += [both[:GROUP, :HEAD_WIDTH], both[GROUP:, HEAD_WIDTH:]]
        own_rounded = own_weight.astype(jnp.bfloat16).astype(jnp.float32)
        added = own_rounded.reshape(WIDE, GROUP, 1) * new_values[r]
        blended = jnp.concatenate(parts, axis=0) + added.reshape(WIDE * GROUP, HEAD_WIDTH)
        at = r * WIDE * GROUP
        final[at : at + WIDE * GROUP, :] = blended * (1.0 / totals)

    for h in range(WIDE * GROUP):
        rows = final[pl.ds(h, ROWS, stride=WIDE * GROUP), :]
        out_ref[:, h * HEAD_WIDTH : (h + 1) * HEAD_WIDTH] = rows.astype(jnp.bfloat16)

    for c in range(CHUNKS):
        for k in range(WIDE // 2):
            across(c, 2 * k + lax.rem(me, 2)).wait_send()
        for d in range(1, 4):
            along(c, d).wait_send()
    for p in range(2):
        for d in range(1, WIDE):
            deliver(d, p, me).wait_send()


def fused(
    hidden_rows, query_weight, key_value_weight, cache_keys, earlier_values, lengths, positions
):
    features = hidden_rows.shape[1]
    dma = pltpu.SemaphoreType.DMA
    vmem, anywhere, smem = (pl.BlockSpec(memory_space=s) for s in (pltpu.VMEM, pl.ANY, pltpu.SMEM))
    return pl.pallas_call(
        kernel,
        out_shape=jax.ShapeDtypeStruct((ROWS, WIDE * GROUP * HEAD_WIDTH), jnp.bfloat16),
        in_specs=[vmem, anywhere, anywhere, anywhere, anywhere, smem, smem],
        out_specs=vmem,
        scratch_shapes=[
            pltpu.VMEM((WIDE, 16, features // 2), jnp.bfloat16),
            pltpu.VMEM((features, GROUP * HEAD_WIDTH), jnp.bfloat16),
            pltpu.VMEM((features, 2 * HEAD_WIDTH), jnp.bfloat16),
            pltpu.VMEM((ROWS, SLOTS, WIDE * HEAD_WIDTH), jnp.bfloat16),
            pltpu.VMEM((ROWS, SLOTS, WIDE * HEAD_WIDTH), jnp.bfloat16),
            pltpu.VMEM((8 * WIDE, features), jnp.bfloat16),
            pltpu.VMEM((HEADS * 64, HEAD_WIDTH), jnp.float32),
            pltpu.VMEM((HEADS * 32, HEAD_WIDTH), jnp.float32),
            pltpu.VMEM((HEADS * 32, HEAD_WIDTH), jnp.float32),
            pltpu.VMEM((WIDE * PACK, HEAD_WIDTH), jnp.float32),
            pltpu.VMEM((WIDE, PACK, HEAD_WIDTH), jnp.bfloat16),
            pltpu.VMEM((WIDE, PACK, HEAD_WIDTH), jnp.bfloat16),
            pltpu.VMEM((2, 8, 128), jnp.float32),
            pltpu.VMEM((ROWS * WIDE * GROUP, HEAD_WIDTH), jnp.float32),
            dma, dma, dma((CHUNKS, 4)), dma((CHUNKS, WIDE)), dma((CHUNKS, WIDE)),
            dma((CHUNKS, 2, 2)), dma, dma,
            dma((2,)), dma((2,)), dma((WIDE, 2)), dma((WIDE, 2)),
        ],
        compiler_params=pltpu.CompilerParams(
            collective_id=0, has_side_effects=True, vmem_limit_bytes=56 * 1024 * 1024
        ),
    )(
        hidden_rows, query_weight, key_value_weight, cache_keys, earlier_values, lengths,
        positions,
    )


def solution(mesh):
    body = fused if mesh.shape["wide"] == WIDE and mesh.shape["narrow"] == 2 else shards
    in_specs = (
        P(("rep", "wide"), "narrow"),
        P("narrow", "wide"),
        P("narrow", "wide"),
        P(("rep", "wide", "narrow"), None, None),
        P(("rep", "wide", "narrow"), None, None),
        P(("rep", "wide", "narrow")),
        P(("rep", "wide", "narrow")),
    )
    out_specs = P(("rep", "wide", "narrow"), None)
    return jax.shard_map(body, mesh=mesh, in_specs=in_specs, out_specs=out_specs, check_vma=False)
```
